32 devices in a mesh: fsdp: 8 (over y, x, core), seq: 4 (over z).
Axes of the slice: x: 2, y: 2, z: 4, core: 2. Of those that a mesh axis runs over, the one named last changes fastest.
Arguments:
- block_in: bfloat16 [20480, 640], P(('fsdp', 'seq')), may hold values from -134 to 134
- query_weight: bfloat16 [640, 1024], P('fsdp'), may hold values from -0.25 to 0.25
- key_weight: bfloat16 [640, 256], P('fsdp'), may hold values from -0.25 to 0.25
- value_weight: bfloat16 [640, 256], P('fsdp'), may hold values from -0.25 to 0.25
- output_weight: bfloat16 [1024, 640], P('fsdp'), may hold values from -0.1875 to 0.1875
- gate_weight: bfloat16 [640, 2048], P('fsdp'), may hold values from -0.25 to 0.25
- up_weight: bfloat16 [640, 2048], P('fsdp'), may hold values from -0.25 to 0.25
- down_weight: bfloat16 [2048, 640], P('fsdp'), may hold values from -0.125 to 0.125
- attention_norm: bfloat16 [640], P('fsdp'), may hold values from 0.099609375 to 1.8984375
- query_norm: bfloat16 [256], P('fsdp'), may hold values from 0.099609375 to 1.8984375
- key_norm: bfloat16 [256], P('fsdp'), may hold values from 0.099609375 to 1.8984375
- post_attention_norm: bfloat16 [640], P('fsdp'), may hold values from 0.099609375 to 1.8984375
- feedforward_norm: bfloat16 [640], P('fsdp'), may hold values from 0.099609375 to 1.8984375
- post_feedforward_norm: bfloat16 [640], P('fsdp'), may hold values from 0.099609375 to 1.8984375
- grad_out: bfloat16 [20480, 640], P(('fsdp', 'seq')), may hold values from -6 to 6
Outputs:
- block_out: bfloat16 [20480, 640], P(('fsdp', 'seq'))
- grad_in: bfloat16 [20480, 640], P(('fsdp', 'seq'))
- grad_query_weight: float32 [640, 1024], P('fsdp')
- grad_key_weight: float32 [640, 256], P('fsdp')
- grad_value_weight: float32 [640, 256], P('fsdp')
- grad_output_weight: float32 [1024, 640], P('fsdp')
- grad_gate_weight: float32 [640, 2048], P('fsdp')
- grad_up_weight: float32 [640, 2048], P('fsdp')
- grad_down_weight: float32 [2048, 640], P('fsdp')
- grad_attention_norm: float32 [640], P('fsdp')
- grad_query_norm: float32 [256], P('fsdp')
- grad_key_norm: float32 [256], P('fsdp')
- grad_post_attention_norm: float32 [640], P('fsdp')
- grad_feedforward_norm: float32 [640], P('fsdp')
- grad_post_feedforward_norm: float32 [640], P('fsdp')
The draws below stay inside these ranges and needn't reach their ends.
All inputs are finite; a program needn't handle non-finite values.
Results may differ from the reference program's by a relative error of at most 0.018.
Values may be sent and summed in bfloat16 or wider, within the bound.
A program may use at most 128 MiB of HBM per device.

```python
import math
import jax
import jax.numpy as jnp
from jax import lax

D = 640
H = 4
HD = 256
FF = 2048
LENGTH = 2560
SEQS = 8
TOKENS = 20480


def draw_block_in(key, part):
    row_key, column_key, base_key = jax.random.split(key, 3)
    row_scale = jnp.exp(jax.random.uniform(row_key, (TOKENS, 1), jnp.float32) * math.log(10.0))
    column_scale = jnp.exp(jax.random.uniform(column_key, (1, D), jnp.float32) * math.log(10.0)) / 3.0
    base_values = jnp.clip(jax.random.normal(base_key, (TOKENS, D), jnp.float32), -4.0, 4.0)
    return (base_values * row_scale * column_scale).astype(jnp.bfloat16)


def level_of(own_key, shape, shards, least, largest):
    loudness = 1.0
    for position, blocks in shards:
        heights = jax.random.uniform(jax.random.fold_in(jax.random.fold_in(own_key, 6), position), (blocks,), jnp.float32, least / len(shards), largest / len(shards))
        loudness = loudness * jnp.repeat(jnp.exp(heights), shape[position] // blocks).reshape((-1,) + (1,) * (len(shape) - 1 - position))
    return loudness


def gaussian(key, shape, scale, most, cuts=(), kind=jnp.bfloat16):
    drawn = scale * jax.random.normal(key, shape, jnp.float32)
    if cuts:
        drawn = drawn * level_of(key, shape, cuts, -0.22, 0.18)
    return jnp.clip(drawn, -most, most).astype(kind)


def setup_inputs(seed: int = 0) -> dict:
    arg_keys = jax.random.split(jax.random.key(seed), 16)
    return {
        "block_in": draw_block_in(jax.random.fold_in(arg_keys[15], 71), 0),
        "query_weight": gaussian(arg_keys[1], (D, H * HD), D ** -0.5, 0.25, ((0, 8),)),
        "key_weight": gaussian(arg_keys[2], (D, HD), D ** -0.5, 0.25, ((0, 8),)),
        "value_weight": gaussian(arg_keys[3], (D, HD), D ** -0.5, 0.25, ((0, 8),)),
        "output_weight": gaussian(arg_keys[4], (H * HD, D), (H * HD) ** -0.5, 0.1875, ((0, 8),)),
        "gate_weight": gaussian(arg_keys[5], (D, FF), D ** -0.5, 0.25, ((0, 8),)),
        "up_weight": gaussian(arg_keys[6], (D, FF), D ** -0.5, 0.25, ((0, 8),)),
        "down_weight": gaussian(arg_keys[7], (FF, D), FF ** -0.5, 0.125, ((0, 8),)),
        "attention_norm": jnp.clip(1.0 + 0.18 * jax.random.normal(arg_keys[8], (D,), jnp.float32), 0.099609375, 1.8984375).astype(jnp.bfloat16),
        "query_norm": jnp.clip(1.0 + 0.18 * jax.random.normal(arg_keys[9], (HD,), jnp.float32), 0.099609375, 1.8984375).astype(jnp.bfloat16),
        "key_norm": jnp.clip(1.0 + 0.18 * jax.random.normal(arg_keys[10], (HD,), jnp.float32), 0.099609375, 1.8984375).astype(jnp.bfloat16),
        "post_attention_norm": jnp.clip(1.0 + 0.18 * jax.random.normal(arg_keys[11], (D,), jnp.float32), 0.099609375, 1.8984375).astype(jnp.bfloat16),
        "feedforward_norm": jnp.clip(1.0 + 0.18 * jax.random.normal(arg_keys[12], (D,), jnp.float32), 0.099609375, 1.8984375).astype(jnp.bfloat16),
        "post_feedforward_norm": jnp.clip(1.0 + 0.18 * jax.random.normal(arg_keys[13], (D,), jnp.float32), 0.099609375, 1.8984375).astype(jnp.bfloat16),
        "grad_out": gaussian(arg_keys[14], (TOKENS, D), 1.0, 6.0, ((0, 32),)),
    }


epsilon = 1e-06
rope_base = 1000000.0
negative = -1e+30

@jax.custom_vjp
def low(v):
    return lax.optimization_barrier(v.astype(jnp.bfloat16)).astype(jnp.float32)

@jax.custom_vjp
def low_back(v):
    return v

def low_keep(v):
    return (low(v), None)

def low_pass(kept, grad):
    return (grad,)

def back_keep(v):
    return (v, None)

def back_low(kept, grad):
    return (low(grad),)
low.defvjp(low_keep, low_pass)
low_back.defvjp(back_keep, back_low)

def product(left, right):
    return jnp.dot(left, right, precision=lax.Precision.HIGHEST, preferred_element_type=jnp.float32)

def rms_scale(values, gain_row):
    return values * lax.rsqrt(lax.optimization_barrier(jnp.mean(values * values, -1, keepdims=True)) + epsilon) * gain_row

def rotate(values, cosine_table, sine_table):
    half_width = values.shape[-1] // 2
    first_half = values[..., :half_width]
    second = values[..., half_width:]
    return jnp.concatenate([first_half * cosine_table - second * sine_table, second * cosine_table + first_half * sine_table], -1)

def angles_for(positions, width):
    half_width = width // 2
    frequency = rope_base ** (-(jnp.arange(half_width).astype(jnp.float32) * 2.0 / width))
    angles = positions[:, None] * frequency[None, :]
    return (jnp.cos(angles), jnp.sin(angles))

def attention(queries, key_rows, value_rows):
    length = key_rows.shape[0]
    block_rows = min(512, length)
    score_scale = queries.shape[-1] ** (-0.5)
    key_pos = jnp.arange(length, dtype=jnp.int32)

    def one_block(block_index):
        row_start = (block_index * block_rows).astype(jnp.int32)
        query_rows = lax.dynamic_slice_in_dim(queries, row_start, block_rows, 0)
        scores = jnp.einsum('qhd,kd->hqk', query_rows, key_rows, precision=lax.Precision.HIGHEST) * score_scale
        scores = low_back(scores)
        query_pos = row_start + jnp.arange(block_rows, dtype=jnp.int32)
        allowed = key_pos[None, :] <= query_pos[:, None]
        scores = jnp.where(allowed[None], scores, negative)
        row_max = lax.optimization_barrier(jnp.max(scores, -1, keepdims=True))
        exp_scores = jnp.exp(scores - row_max)
        weights = low(exp_scores / lax.optimization_barrier(jnp.sum(exp_scores, -1, keepdims=True)))
        return jnp.einsum('hqk,kd->qhd', weights, value_rows, precision=lax.Precision.HIGHEST)
    blocks = lax.map(jax.checkpoint(one_block), jnp.arange(length // block_rows, dtype=jnp.int32))
    return blocks.reshape(queries.shape)

def forward(seq_in, query_weight, key_weight, value_weight, output_weight, gate_weight, up_weight, down_weight, attention_norm, query_norm, key_norm, post_attention_norm, feedforward_norm, post_feedforward_norm):
    length = seq_in.shape[0]
    head_size = query_norm.shape[0]
    head_count = query_weight.shape[1] // head_size
    cosine_table, sine_table = angles_for(jnp.arange(length).astype(jnp.float32), head_size)
    normed = low(rms_scale(seq_in, attention_norm))
    query_lin = low_back(product(normed, query_weight)).reshape(length, head_count, head_size)
    key_lin = low_back(product(normed, key_weight))
    value_rows = low(low_back(product(normed, value_weight)))
    queries = low(low_back(rotate(rms_scale(query_lin, query_norm), cosine_table[:, None, :], sine_table[:, None, :])))
    key_rows = low(low_back(rotate(rms_scale(key_lin, key_norm), cosine_table, sine_table)))
    mixed = low(low_back(attention(queries, key_rows, value_rows).reshape(length, head_count * head_size)))
    attended = low_back(product(mixed, output_weight))
    residual = seq_in + rms_scale(attended, post_attention_norm)
    normed_second = low(rms_scale(residual, feedforward_norm))
    gate_lin = low_back(product(normed_second, gate_weight))
    up_lin = low_back(product(normed_second, up_weight))
    activated = low(jax.nn.gelu(gate_lin, approximate=True) * up_lin)
    down_lin = low_back(product(activated, down_weight))
    return residual + rms_scale(down_lin, post_feedforward_norm)

def reference(block_in, query_weight, key_weight, value_weight, output_weight, gate_weight, up_weight, down_weight, attention_norm, query_norm, key_norm, post_attention_norm, feedforward_norm, post_feedforward_norm, grad_out):
    params = tuple((weight.astype(jnp.float32) for weight in (query_weight, key_weight, value_weight, output_weight, gate_weight, up_weight, down_weight, attention_norm, query_norm, key_norm, post_attention_norm, feedforward_norm, post_feedforward_norm)))
    seq_inputs = block_in.astype(jnp.float32).reshape(SEQS, LENGTH, D)
    seq_grads = grad_out.astype(jnp.float32).reshape(SEQS, LENGTH, D)

    def one_sequence(totals, pair):
        seq_in, seq_grad = pair
        result, pullback = jax.vjp(forward, seq_in, *params)
        grads = pullback(seq_grad)
        new_totals = tuple((running + fresh for running, fresh in zip(totals, grads[1:])))
        return (new_totals, (result, grads[0]))
    start_totals = tuple((jnp.zeros(weight.shape, jnp.float32) for weight in params))
    totals, (results, input_grads) = lax.scan(one_sequence, start_totals, (seq_inputs, seq_grads))
    block_out = results.reshape(TOKENS, D).astype(jnp.bfloat16)
    grad_in = input_grads.reshape(TOKENS, D).astype(jnp.bfloat16)
    return (block_out, grad_in, totals[0], totals[1], totals[2], totals[3], totals[4], totals[5], totals[6], totals[7], totals[8], totals[9], totals[10], totals[11], totals[12])
```

```python
import functools
import math

import jax
import jax.numpy as jnp
from jax import lax
from jax.experimental import pallas as pl
from jax.experimental.pallas import tpu as pltpu
from jax.sharding import PartitionSpec as P

epsilon = 1e-06
rope_base = 1000000.0


def rms_scale(values, gain_row):
    return values * lax.rsqrt(jnp.mean(values * values, -1, keepdims=True) + epsilon) * gain_row


def rotate(values, cosine_table, sine_table):
    half_width = values.shape[-1] // 2
    first_half = values[..., :half_width]
    second = values[..., half_width:]
    return jnp.concatenate(
        [
            first_half * cosine_table - second * sine_table,
            second * cosine_table + first_half * sine_table,
        ],
        -1,
    )


def angles_for(positions, width):
    half_width = width // 2
    frequency = rope_base ** (-(jnp.arange(half_width).astype(jnp.float32) * 2.0 / width))
    angles = positions[:, None] * frequency[None, :]
    return (jnp.cos(angles), jnp.sin(angles))


def gelu_product(gate_lin, up_lin):
    return jax.nn.gelu(gate_lin, approximate=True) * up_lin


def bit_count(axis):
    return lax.axis_size(axis).bit_length() - 1


def my_bit(axis, bit):
    return (lax.axis_index(axis) >> bit) & 1


def flip_pairs(axis, bit):
    return [(i, i ^ (1 << bit)) for i in range(lax.axis_size(axis))]


def gather_order(axis, forward):
    upper = list(range(1, bit_count(axis)))
    return (upper if forward else upper[::-1]) + [0]


def gather_rows(block, forward):
    axis = "fsdp"
    bits = bit_count(axis)
    grid_shape = (2,) * bits
    buffer = jnp.zeros(grid_shape + block.shape, block.dtype)
    tail = (0,) * block.ndim
    own = [my_bit(axis, bits - 1 - d) for d in range(bits)]
    buffer = lax.dynamic_update_slice(
        buffer, block.reshape((1,) * bits + block.shape), tuple(own) + tail
    )
    piece = block.reshape((1,) * bits + block.shape)
    done = set()
    for step, bit in enumerate(gather_order(axis, forward)):
        if step:
            starts = [0 if bits - 1 - d in done else own[d] for d in range(bits)]
            sizes = tuple(2 if bits - 1 - d in done else 1 for d in range(bits))
            piece = lax.dynamic_slice(buffer, tuple(starts) + tail, sizes + block.shape)
        arrived = lax.ppermute(piece, axis, flip_pairs(axis, bit))
        starts = [0 if bits - 1 - d in done else own[d] for d in range(bits)]
        starts[bits - 1 - bit] = 1 - own[bits - 1 - bit]
        buffer = lax.dynamic_update_slice(buffer, arrived, tuple(starts) + tail)
        done.add(bit)
    return buffer.reshape((-1,) + block.shape)


def scatter_rows(values, forward):
    axis = "fsdp"
    bits = bit_count(axis)
    block_shape = values.shape[1:]
    buffer = values.astype(jnp.bfloat16).reshape((2,) * bits + block_shape)
    for bit in gather_order(axis, forward)[::-1]:
        dim = bits - 1 - bit
        mine = my_bit(axis, bit)
        kept = lax.dynamic_slice_in_dim(buffer, mine, 1, dim)
        sent = lax.dynamic_slice_in_dim(buffer, 1 - mine, 1, dim)
        arrived = lax.ppermute(sent, axis, flip_pairs(axis, bit))
        total = kept.astype(jnp.float32) + arrived.astype(jnp.float32)
        buffer = total.astype(jnp.bfloat16)
    return buffer.reshape(block_shape)


def seq_sum(shard):
    axis = "seq"
    count = lax.axis_size(axis)
    me = lax.axis_index(axis)
    dim = 1 if shard.shape[1] % (128 * count) == 0 else 0
    width = shard.shape[dim] // count
    total = lax.dynamic_slice_in_dim(shard, me * width, width, dim).astype(jnp.float32)
    for shift in range(1, count):
        to = (me + shift) % count
        sent = lax.dynamic_slice_in_dim(shard, to * width, width, dim)
        pairs = [(i, (i + shift) % count) for i in range(count)]
        total = total + lax.ppermute(sent, axis, pairs).astype(jnp.float32)
    part = total.astype(jnp.bfloat16)
    result = lax.dynamic_update_slice_in_dim(jnp.zeros_like(shard), part, me * width, dim)
    for shift in range(1, count):
        pairs = [(i, (i + shift) % count) for i in range(count)]
        arrived = lax.ppermute(part, axis, pairs)
        result = lax.dynamic_update_slice_in_dim(
            result, arrived, ((me - shift + count) % count) * width, dim
        )
    return result


def dims(left, right):
    return (((left,), (right,)), ((), ()))


def f32_dot(left, right, left_dim, right_dim):
    return lax.dot_general(
        left, right, dims(left_dim, right_dim), preferred_element_type=jnp.float32
    )


def forward_kernel(slots, key_tile, factor, place_ref, query_ref, *refs):
    kv_refs = refs[:slots]
    out_ref, total_ref, sum_ref, acc_ref = refs[slots:]
    rows, width = query_ref.shape
    sum_ref[...] = jnp.zeros_like(sum_ref)
    acc_ref[...] = jnp.zeros_like(acc_ref)

    def tile(kv_ref, start, masked):
        keys = kv_ref[pl.ds(start, key_tile), :width]
        values = kv_ref[pl.ds(start, key_tile), width:]
        weights = jnp.exp2(f32_dot(keys, query_ref[...], 1, 1) * factor)
        if masked:
            key_pos = start + lax.broadcasted_iota(jnp.int32, weights.shape, 0)
            query_pos = lax.broadcasted_iota(jnp.int32, weights.shape, 1)
            weights = jnp.where(key_pos <= query_pos, weights, 0.0)
        sum_ref[...] += jnp.sum(weights, 0, keepdims=True)
        acc_ref[...] += f32_dot(values, weights.astype(jnp.bfloat16), 0, 0)

    for slot in range(slots):

        @pl.when(slot <= place_ref[0])
        def _(slot=slot):
            for start in range(0, rows, key_tile):
                tile(kv_refs[slot], start, slot == 0)

    total = sum_ref[...]
    total_ref[...] = total[None]
    out_ref[...] = (acc_ref[...] / total).T.astype(out_ref.dtype)


def attend_forward(place, query, kv_list, heads):
    rows = query.shape[0]
    width = query.shape[1] // heads
    slots = len(kv_list)
    kernel = functools.partial(
        forward_kernel, slots, rows // 2, math.log2(math.e) * width**-0.5
    )
    return pl.pallas_call(
        kernel,
        grid_spec=pltpu.PrefetchScalarGridSpec(
            num_scalar_prefetch=1,
            grid=(heads,),
            in_specs=[pl.BlockSpec((rows, width), lambda h, p: (0, h))]
            + [pl.BlockSpec((rows, 2 * width), lambda h, p: (0, 0))] * slots,
            out_specs=[
                pl.BlockSpec((rows, width), lambda h, p: (0, h)),
                pl.BlockSpec((1, 1, rows), lambda h, p: (h, 0, 0)),
            ],
            scratch_shapes=[
                pltpu.VMEM((1, rows), jnp.float32),
                pltpu.VMEM((width, rows), jnp.float32),
            ],
        ),
        out_shape=[
            jax.ShapeDtypeStruct(query.shape, jnp.bfloat16),
            jax.ShapeDtypeStruct((heads, 1, rows), jnp.float32),
        ],
        compiler_params=pltpu.CompilerParams(vmem_limit_bytes=40 * 2**20),
        cost_estimate=pl.CostEstimate(
            flops=4 * slots * heads * rows * rows * width,
            bytes_accessed=8 * rows * width * heads,
            transcendentals=slots * heads * rows * rows,
        ),
    )(place, query, *kv_list)


def backward_kernel(slots, key_tile, factor, scale, place_ref, query_ref, grad_ref, *refs):
    log_ref, delta_ref = refs[:2]
    kv_refs = refs[2 : 2 + slots]
    query_grad_ref = refs[2 + slots]
    kv_grad_refs = refs[3 + slots : 3 + 2 * slots]
    acc_ref, total_ref = refs[3 + 2 * slots :]
    rows, width = query_ref.shape
    head = pl.program_id(0)

    @pl.when(head == 0)
    def _():
        total_ref[...] = jnp.zeros_like(total_ref)

    acc_ref[...] = jnp.zeros_like(acc_ref)

    def tile(slot, start, masked):
        kv_ref = kv_refs[slot]
        here = pl.ds(start, key_tile)
        keys = kv_ref[here, :width]
        values = kv_ref[here, width:]
        weights = jnp.exp2(f32_dot(keys, query_ref[...], 1, 1) * factor - log_ref[0])
        if masked:
            key_pos = start + lax.broadcasted_iota(jnp.int32, weights.shape, 0)
            query_pos = lax.broadcasted_iota(jnp.int32, weights.shape, 1)
            weights = jnp.where(key_pos <= query_pos, weights, 0.0)
        grad_weights = f32_dot(values, grad_ref[...], 1, 1)
        grad_scores = (weights * (grad_weights - delta_ref[0])).astype(jnp.bfloat16)
        total_ref[slot, here, width:] += f32_dot(
            weights.astype(jnp.bfloat16), grad_ref[...], 1, 0
        )
        total_ref[slot, here, :width] += f32_dot(grad_scores, query_ref[...], 1, 0)
        acc_ref[...] += f32_dot(grad_scores, keys, 0, 0)

    for slot in range(slots):

        @pl.when(slot <= place_ref[0])
        def _(slot=slot):
            for start in range(0, rows, key_tile):
                tile(slot, start, slot == 0)

    query_grad_ref[...] = (acc_ref[...] * scale).astype(query_grad_ref.dtype)

    @pl.when(head == pl.num_programs(0) - 1)
    def _():
        for slot in range(slots):
            kv_grad_refs[slot][:, :width] = (total_ref[slot, :, :width] * scale).astype(
                jnp.bfloat16
            )
            kv_grad_refs[slot][:, width:] = total_ref[slot, :, width:].astype(jnp.bfloat16)


def attend_backward(place, query, grad_rows, log_totals, delta, kv_list, heads):
    rows = query.shape[0]
    width = query.shape[1] // heads
    slots = len(kv_list)
    scale = width**-0.5
    kernel = functools.partial(
        backward_kernel, slots, rows // 2, math.log2(math.e) * scale, scale
    )
    head_spec = pl.BlockSpec((rows, width), lambda h, p: (0, h))
    line_spec = pl.BlockSpec((1, 1, rows), lambda h, p: (h, 0, 0))
    kv_spec = pl.BlockSpec((rows, 2 * width), lambda h, p: (0, 0))
    return pl.pallas_call(
        kernel,
        grid_spec=pltpu.PrefetchScalarGridSpec(
            num_scalar_prefetch=1,
            grid=(heads,),
            in_specs=[head_spec, head_spec, line_spec, line_spec] + [kv_spec] * slots,
            out_specs=[head_spec] + [kv_spec] * slots,
            scratch_shapes=[
                pltpu.VMEM((rows, width), jnp.float32),
                pltpu.VMEM((slots, rows, 2 * width), jnp.float32),
            ],
        ),
        out_shape=[jax.ShapeDtypeStruct(query.shape, jnp.bfloat16)]
        + [jax.ShapeDtypeStruct((rows, 2 * width), jnp.bfloat16)] * slots,
        compiler_params=pltpu.CompilerParams(vmem_limit_bytes=48 * 2**20),
        cost_estimate=pl.CostEstimate(
            flops=10 * slots * heads * rows * rows * width,
            bytes_accessed=12 * rows * width * heads,
            transcendentals=slots * heads * rows * rows,
        ),
    )(place, query, grad_rows, log_totals, delta, *kv_list)


def up_pairs(shift):
    return [(i, i + shift) for i in range(lax.axis_size("seq") - shift)]


def down_pairs(shift):
    return [(i + shift, i) for i in range(lax.axis_size("seq") - shift)]


def mm(left, right):
    return jnp.dot(left, right, preferred_element_type=jnp.float32)


def mm_nt(left, right):
    return f32_dot(left, right, 1, 1)


def mm_tn(left, right):
    return f32_dot(left, right, 0, 0)


def per_device(
    block_in,
    query_weight,
    key_weight,
    value_weight,
    output_weight,
    gate_weight,
    up_weight,
    down_weight,
    attention_norm,
    query_norm,
    key_norm,
    post_attention_norm,
    feedforward_norm,
    post_feedforward_norm,
    grad_out,
):
    parts = lax.axis_size("fsdp")
    gains = (
        attention_norm,
        query_norm,
        key_norm,
        post_attention_norm,
        feedforward_norm,
        post_feedforward_norm,
    )
    gain_sizes = [g.shape[0] for g in gains]
    gain_total = sum(gain_sizes)
    kv_rows, kv_width = key_weight.shape[0], 2 * key_weight.shape[1]
    kv_block = jnp.concatenate([key_weight, value_weight], 1)
    extra_rows = 16
    gain_block = jnp.concatenate(
        gains + (jnp.zeros((extra_rows * kv_width - gain_total,), jnp.bfloat16),)
    ).reshape(extra_rows, kv_width)
    kv_gathered = gather_rows(jnp.concatenate([kv_block, gain_block], 0), False)
    query_full = gather_rows(query_weight, True).reshape(-1, query_weight.shape[1])
    kv_full = kv_gathered[:, :kv_rows].reshape(-1, kv_width)
    gain_rows = kv_gathered[:, kv_rows:].reshape(parts, -1).astype(jnp.float32)
    split_gains = []
    offset = 0
    for size in gain_sizes:
        split_gains.append(gain_rows[:, offset : offset + size].reshape(-1))
        offset += size
    attention_gain, query_gain, key_gain, post_attention_gain, second_gain, post_second_gain = (
        split_gains
    )
    output_full = gather_rows(output_weight, True).reshape(-1, output_weight.shape[1])
    up_full = gather_rows(up_weight, False).reshape(-1, up_weight.shape[1])
    gate_full = gather_rows(gate_weight, True).reshape(-1, gate_weight.shape[1])
    down_full = gather_rows(down_weight, False).reshape(-1, down_weight.shape[1])

    token_count = block_in.shape[0]
    head_size = query_gain.shape[0]
    head_count = query_full.shape[1] // head_size
    slots = lax.axis_size("seq")
    seq_place = lax.axis_index("seq")
    place = seq_place.astype(jnp.int32).reshape(1)
    input_f = block_in.astype(jnp.float32)
    normed, pull_normed = jax.vjp(rms_scale, input_f, attention_gain)
    normed_low = normed.astype(jnp.bfloat16)
    kv_lin = mm(normed_low, kv_full)
    key_lin = kv_lin[:, :head_size]
    value_low = kv_lin[:, head_size:].astype(jnp.bfloat16)
    positions = (seq_place * token_count + jnp.arange(token_count, dtype=jnp.int32)).astype(
        jnp.float32
    )
    cosine_table, sine_table = angles_for(positions, head_size)

    def query_piece(values, gain_row):
        return rotate(rms_scale(values, gain_row), cosine_table[:, None, :], sine_table[:, None, :])

    def key_piece(values, gain_row):
        return rotate(rms_scale(values, gain_row), cosine_table, sine_table)

    key_rows, pull_keys = jax.vjp(key_piece, key_lin, key_gain)
    kv_own = jnp.concatenate([key_rows.astype(jnp.bfloat16), value_low], 1)
    kv_list = [kv_own] + [lax.ppermute(kv_own, "seq", up_pairs(s)) for s in range(1, slots)]
    query_lin = mm(normed_low, query_full).reshape(token_count, head_count, head_size)
    queries, pull_queries = jax.vjp(query_piece, query_lin, query_gain)
    queries_low = queries.astype(jnp.bfloat16).reshape(token_count, head_count * head_size)
    mixed, totals = attend_forward(place, queries_low, kv_list, head_count)
    attended = mm(mixed, output_full)
    post_branch, pull_post = jax.vjp(rms_scale, attended, post_attention_gain)
    residual = input_f + post_branch
    normed_second, pull_second = jax.vjp(rms_scale, residual, second_gain)
    second_low = normed_second.astype(jnp.bfloat16)
    gate_lin = mm(second_low, gate_full)
    up_lin = mm(second_low, up_full)
    activated, pull_activated = jax.vjp(gelu_product, gate_lin, up_lin)
    activated_low = activated.astype(jnp.bfloat16)
    down_lin = mm(activated_low, down_full)
    tail_branch, pull_tail = jax.vjp(rms_scale, down_lin, post_second_gain)
    block_out = (residual + tail_branch).astype(jnp.bfloat16)
    grad_f = grad_out.astype(jnp.float32)
    grad_down, grad_post_second = pull_tail(grad_f)
    grad_down_low = grad_down.astype(jnp.bfloat16)

    def reduced(left, right, forward):
        product = mm_tn(left, right).astype(jnp.bfloat16)
        return scatter_rows(product.reshape(parts, -1, product.shape[1]), forward)

    sum_down = reduced(activated_low, grad_down_low, False)
    grad_activated = mm_nt(grad_down_low, down_full)
    grad_gate, grad_up = pull_activated(grad_activated)
    gate_low = grad_gate.astype(jnp.bfloat16)
    up_low = grad_up.astype(jnp.bfloat16)
    sum_gate = reduced(second_low, gate_low, True)
    sum_up = reduced(second_low, up_low, False)
    grad_second = mm_nt(gate_low, gate_full) + mm_nt(up_low, up_full)
    grad_resid_part, grad_second_gain = pull_second(grad_second)
    grad_residual = grad_f + grad_resid_part
    grad_attended, grad_post_attention = pull_post(grad_residual)
    attended_low = grad_attended.astype(jnp.bfloat16)
    sum_output = reduced(mixed, attended_low, True)
    grad_mixed = mm_nt(attended_low, output_full).astype(jnp.bfloat16)
    delta = jnp.sum(
        (grad_mixed.astype(jnp.float32) * mixed.astype(jnp.float32)).reshape(
            token_count, head_count, head_size
        ),
        -1,
    ).T.reshape(head_count, 1, token_count)
    outs = attend_backward(
        place, queries_low, grad_mixed, jnp.log2(totals), delta, kv_list, head_count
    )
    grad_queries, kv_grads = outs[0], outs[1:]
    kv_grad = kv_grads[0].astype(jnp.float32)
    for shift in range(1, slots):
        arrived = lax.ppermute(kv_grads[shift], "seq", down_pairs(shift))
        kv_grad = kv_grad + arrived.astype(jnp.float32)
    kv_grad = kv_grad.astype(jnp.bfloat16)
    grad_query_lin, grad_query_gain = pull_queries(
        grad_queries.astype(jnp.float32).reshape(query_lin.shape)
    )
    query_lin_low = grad_query_lin.reshape(token_count, head_count * head_size).astype(jnp.bfloat16)
    sum_query = reduced(normed_low, query_lin_low, True)
    grad_normed = mm_nt(query_lin_low, query_full)
    grad_key_lin, grad_key_gain = pull_keys(kv_grad[:, :head_size].astype(jnp.float32))
    kv_lin_low = jnp.concatenate(
        [grad_key_lin.astype(jnp.bfloat16), kv_grad[:, head_size:]], 1
    )
    grad_normed = grad_normed + mm_nt(kv_lin_low, kv_full)
    grad_input_part, grad_attention_gain = pull_normed(grad_normed)
    grad_in = (grad_residual + grad_input_part).astype(jnp.bfloat16)
    gain_grads = (
        grad_attention_gain,
        grad_query_gain,
        grad_key_gain,
        grad_post_attention,
        grad_second_gain,
        grad_post_second,
    )
    gain_grad_rows = jnp.concatenate(
        [g.astype(jnp.bfloat16).reshape(parts, -1) for g in gain_grads]
        + [jnp.zeros((parts, extra_rows * kv_width - gain_total), jnp.bfloat16)],
        1,
    ).reshape(parts, extra_rows, kv_width)
    kv_product = mm_tn(normed_low, kv_lin_low).astype(jnp.bfloat16).reshape(
        parts, kv_rows, kv_width
    )
    sum_kv = scatter_rows(jnp.concatenate([kv_product, gain_grad_rows], 1), False)

    down_sum = seq_sum(sum_down).astype(jnp.float32)
    gate_sum = seq_sum(sum_gate).astype(jnp.float32)
    up_sum = seq_sum(sum_up).astype(jnp.float32)
    output_sum = seq_sum(sum_output).astype(jnp.float32)
    query_sum = seq_sum(sum_query).astype(jnp.float32)
    kv_sum = seq_sum(sum_kv).astype(jnp.float32)
    gain_sum = kv_sum[kv_rows:].reshape(-1)
    gain_outs = []
    offset = 0
    for size in gain_sizes:
        gain_outs.append(gain_sum[offset : offset + size])
        offset += size
    return (
        block_out,
        grad_in,
        query_sum,
        kv_sum[:kv_rows, :head_size],
        kv_sum[:kv_rows, head_size:],
        output_sum,
        gate_sum,
        up_sum,
        down_sum,
        *gain_outs,
    )


def solution(mesh):
    in_specs = (
        P(("fsdp", "seq"), None),
        P("fsdp", None),
        P("fsdp", None),
        P("fsdp", None),
        P("fsdp", None),
        P("fsdp", None),
        P("fsdp", None),
        P("fsdp", None),
        P("fsdp"),
        P("fsdp"),
        P("fsdp"),
        P("fsdp"),
        P("fsdp"),
        P("fsdp"),
        P(("fsdp", "seq"), None),
    )
    out_specs = (
        P(("fsdp", "seq"), None),
        P(("fsdp", "seq"), None),
        P("fsdp", None),
        P("fsdp", None),
        P("fsdp", None),
        P("fsdp", None),
        P("fsdp", None),
        P("fsdp", None),
        P("fsdp", None),
        P("fsdp"),
        P("fsdp"),
        P("fsdp"),
        P("fsdp"),
        P("fsdp"),
        P("fsdp"),
    )
    return jax.shard_map(
        per_device, mesh=mesh, in_specs=in_specs, out_specs=out_specs, check_vma=False
    )
```

```python
import functools
import math

import jax
import jax.numpy as jnp
from jax import lax
from jax.experimental import pallas as pl
from jax.experimental.pallas import tpu as pltpu
from jax.sharding import PartitionSpec as P

epsilon = 1e-06
rope_base = 1000000.0


def rms_scale(values, gain_row):
    return values * lax.rsqrt(jnp.mean(values * values, -1, keepdims=True) + epsilon) * gain_row


def rotate(values, cosine_table, sine_table):
    half_width = values.shape[-1] // 2
    first_half = values[..., :half_width]
    second = values[..., half_width:]
    return jnp.concatenate(
        [
            first_half * cosine_table - second * sine_table,
            second * cosine_table + first_half * sine_table,
        ],
        -1,
    )


def angles_for(positions, width):
    half_width = width // 2
    frequency = rope_base ** (-(jnp.arange(half_width).astype(jnp.float32) * 2.0 / width))
    angles = positions[:, None] * frequency[None, :]
    return (jnp.cos(angles), jnp.sin(angles))


def gelu_product(gate_lin, up_lin):
    return jax.nn.gelu(gate_lin, approximate=True) * up_lin


def bit_count(axis):
    return lax.axis_size(axis).bit_length() - 1


def my_bit(axis, bit):
    return (lax.axis_index(axis) >> bit) & 1


def flip_pairs(axis, bit):
    return [(i, i ^ (1 << bit)) for i in range(lax.axis_size(axis))]


def gather_order(axis, forward):
    upper = list(range(1, bit_count(axis)))
    return (upper if forward else upper[::-1]) + [0]


def gather_start(block):
    bits = bit_count("fsdp")
    own = [my_bit("fsdp", bits - 1 - d) for d in range(bits)]
    start = tuple(own) + (0,) * block.ndim
    shaped = block.reshape((1,) * bits + block.shape)
    return lax.dynamic_update_slice(
        jnp.zeros((2,) * bits + block.shape, block.dtype), shaped, start
    )


def gather_step(buffer, order, step):
    axis = "fsdp"
    bits = bit_count(axis)
    bit = order[step]
    done = order[:step]
    block_shape = buffer.shape[bits:]
    tail = (0,) * len(block_shape)
    own = [my_bit(axis, bits - 1 - d) for d in range(bits)]
    starts = [0 if bits - 1 - d in done else own[d] for d in range(bits)]
    sizes = tuple(2 if bits - 1 - d in done else 1 for d in range(bits))
    piece = lax.dynamic_slice(buffer, tuple(starts) + tail, sizes + block_shape)
    arrived = lax.ppermute(piece, axis, flip_pairs(axis, bit))
    starts[bits - 1 - bit] = 1 - own[bits - 1 - bit]
    return lax.dynamic_update_slice(buffer, arrived, tuple(starts) + tail)


def gather_steps(buffer, forward, first, last):
    order = gather_order("fsdp", forward)
    for step in range(len(order))[first:last]:
        buffer = gather_step(buffer, order, step)
    return buffer


def gather_rows(block, forward):
    buffer = gather_steps(gather_start(block), forward, 0, None)
    return buffer.reshape((-1,) + block.shape)


def scatter_start(values):
    bits = bit_count("fsdp")
    return values.astype(jnp.bfloat16).reshape((2,) * bits + values.shape[1:])


def scatter_steps(buffer, forward, first, last):
    axis = "fsdp"
    bits = bit_count(axis)
    for bit in gather_order(axis, forward)[::-1][first:last]:
        dim = bits - 1 - bit
        mine = my_bit(axis, bit)
        kept = lax.dynamic_slice_in_dim(buffer, mine, 1, dim)
        sent = lax.dynamic_slice_in_dim(buffer, 1 - mine, 1, dim)
        arrived = lax.ppermute(sent, axis, flip_pairs(axis, bit))
        total = kept.astype(jnp.float32) + arrived.astype(jnp.float32)
        buffer = total.astype(jnp.bfloat16)
    return buffer


def scatter_end(buffer):
    return buffer.reshape(buffer.shape[bit_count("fsdp") :])


def seq_scatter(shard):
    axis = "seq"
    count = lax.axis_size(axis)
    me = lax.axis_index(axis)
    dim = 1 if shard.shape[1] % (128 * count) == 0 else 0
    width = shard.shape[dim] // count
    total = lax.dynamic_slice_in_dim(shard, me * width, width, dim).astype(jnp.float32)
    for shift in range(1, count):
        to = (me + shift) % count
        sent = lax.dynamic_slice_in_dim(shard, to * width, width, dim)
        pairs = [(i, (i + shift) % count) for i in range(count)]
        total = total + lax.ppermute(sent, axis, pairs).astype(jnp.float32)
    return total.astype(jnp.bfloat16)


def seq_gather(shard, part):
    axis = "seq"
    count = lax.axis_size(axis)
    me = lax.axis_index(axis)
    dim = 1 if shard.shape[1] % (128 * count) == 0 else 0
    width = shard.shape[dim] // count
    result = lax.dynamic_update_slice_in_dim(jnp.zeros_like(shard), part, me * width, dim)
    for shift in range(1, count):
        pairs = [(i, (i + shift) % count) for i in range(count)]
        arrived = lax.ppermute(part, axis, pairs)
        result = lax.dynamic_update_slice_in_dim(
            result, arrived, ((me - shift + count) % count) * width, dim
        )
    return result


def seq_sum(shard):
    return seq_gather(shard, seq_scatter(shard))


def dims(left, right):
    return (((left,), (right,)), ((), ()))


def f32_dot(left, right, left_dim, right_dim):
    return lax.dot_general(
        left, right, dims(left_dim, right_dim), preferred_element_type=jnp.float32
    )


def forward_kernel(own, slots, ties, key_tile, factor, place_ref, query_ref, *refs):
    kv_refs = refs[:slots]
    rows, width = query_ref.shape
    if own:
        acc_out, sum_out, sum_ref, acc_ref = refs[slots + ties :]
        sum_ref[...] = jnp.zeros_like(sum_ref)
        acc_ref[...] = jnp.zeros_like(acc_ref)
    else:
        acc_in, sum_in = refs[slots : slots + 2]
        out_ref, total_ref, sum_ref, acc_ref = refs[slots + 2 + ties :]
        sum_ref[...] = sum_in[0]
        acc_ref[...] = acc_in[0]

    def tile(kv_ref, start, masked):
        keys = kv_ref[pl.ds(start, key_tile), :width]
        values = kv_ref[pl.ds(start, key_tile), width:]
        weights = jnp.exp2(f32_dot(keys, query_ref[...], 1, 1) * factor)
        if masked:
            key_pos = start + lax.broadcasted_iota(jnp.int32, weights.shape, 0)
            query_pos = lax.broadcasted_iota(jnp.int32, weights.shape, 1)
            weights = jnp.where(key_pos <= query_pos, weights, 0.0)
        sum_ref[...] += jnp.sum(weights, 0, keepdims=True)
        acc_ref[...] += f32_dot(values, weights.astype(jnp.bfloat16), 0, 0)

    for slot in range(slots):

        @pl.when((0 if own else slot + 1) <= place_ref[0])
        def _(slot=slot):
            for start in range(0, rows, key_tile):
                tile(kv_refs[slot], start, own)

    total = sum_ref[...]
    if own:
        sum_out[...] = total[None]
        acc_out[...] = acc_ref[...][None]
    else:
        total_ref[...] = total[None]
        out_ref[...] = (acc_ref[...] / total).T.astype(out_ref.dtype)


def attend_forward(place, query, kv_list, heads, before, ties):
    own = before is None
    rows = query.shape[0]
    width = query.shape[1] // heads
    slots = len(kv_list)
    kernel = functools.partial(
        forward_kernel, own, slots, len(ties), rows // 2, math.log2(math.e) * width**-0.5
    )
    head_spec = pl.BlockSpec((rows, width), lambda h, p: (0, h))
    acc_spec = pl.BlockSpec((1, width, rows), lambda h, p: (h, 0, 0))
    line_spec = pl.BlockSpec((1, 1, rows), lambda h, p: (h, 0, 0))
    line_shape = jax.ShapeDtypeStruct((heads, 1, rows), jnp.float32)
    acc_shape = jax.ShapeDtypeStruct((heads, width, rows), jnp.float32)
    return pl.pallas_call(
        kernel,
        grid_spec=pltpu.PrefetchScalarGridSpec(
            num_scalar_prefetch=1,
            grid=(heads,),
            in_specs=[head_spec]
            + [pl.BlockSpec((rows, 2 * width), lambda h, p: (0, 0))] * slots
            + ([] if own else [acc_spec, line_spec])
            + [pl.BlockSpec(memory_space=pl.ANY)] * len(ties),
            out_specs=[acc_spec if own else head_spec, line_spec],
            scratch_shapes=[
                pltpu.VMEM((1, rows), jnp.float32),
                pltpu.VMEM((width, rows), jnp.float32),
            ],
        ),
        out_shape=[
            acc_shape if own else jax.ShapeDtypeStruct(query.shape, jnp.bfloat16),
            line_shape,
        ],
        compiler_params=pltpu.CompilerParams(vmem_limit_bytes=40 * 2**20),
        cost_estimate=pl.CostEstimate(
            flops=8 * slots * heads * rows * rows * width,
            bytes_accessed=8 * rows * width * heads,
            transcendentals=slots * heads * rows * rows,
        ),
    )(place, query, *kv_list, *(before or ()), *ties)


def backward_kernel(own, slots, ties, key_tile, factor, scale, place_ref, query_ref, grad_ref, *refs):
    log_ref, delta_ref = refs[:2]
    kv_refs = refs[2 : 2 + slots]
    if own:
        before_ref = refs[2 + slots]
    refs = refs[: 2 + slots] + refs[2 + slots + ties + (1 if own else 0) :]
    query_grad_ref = refs[2 + slots]
    kv_grad_refs = refs[3 + slots : 3 + 2 * slots]
    acc_ref, total_ref = refs[3 + 2 * slots :]
    rows, width = query_ref.shape
    head = pl.program_id(0)

    @pl.when(head == 0)
    def _():
        total_ref[...] = jnp.zeros_like(total_ref)

    acc_ref[...] = before_ref[...] if own else jnp.zeros_like(acc_ref)

    def tile(slot, start, masked):
        kv_ref = kv_refs[slot]
        here = pl.ds(start, key_tile)
        keys = kv_ref[here, :width]
        values = kv_ref[here, width:]
        weights = jnp.exp2(f32_dot(keys, query_ref[...], 1, 1) * factor - log_ref[0])
        if masked:
            key_pos = start + lax.broadcasted_iota(jnp.int32, weights.shape, 0)
            query_pos = lax.broadcasted_iota(jnp.int32, weights.shape, 1)
            weights = jnp.where(key_pos <= query_pos, weights, 0.0)
        grad_weights = f32_dot(values, grad_ref[...], 1, 1)
        grad_scores = (weights * (grad_weights - delta_ref[0])).astype(jnp.bfloat16)
        total_ref[slot, here, width:] += f32_dot(
            weights.astype(jnp.bfloat16), grad_ref[...], 1, 0
        )
        total_ref[slot, here, :width] += f32_dot(grad_scores, query_ref[...], 1, 0)
        acc_ref[...] += f32_dot(grad_scores, keys, 0, 0)

    for slot in range(slots):

        @pl.when((0 if own else slot + 1) <= place_ref[0])
        def _(slot=slot):
            for start in range(0, rows, key_tile):
                tile(slot, start, own)

    if own:
        query_grad_ref[...] = (acc_ref[...] * scale).astype(query_grad_ref.dtype)
    else:
        query_grad_ref[...] = acc_ref[...]

    @pl.when(head == pl.num_programs(0) - 1)
    def _():
        for slot in range(slots):
            kv_grad_refs[slot][:, :width] = (total_ref[slot, :, :width] * scale).astype(
                jnp.bfloat16
            )
            kv_grad_refs[slot][:, width:] = total_ref[slot, :, width:].astype(jnp.bfloat16)


def attend_backward(place, query, grad_rows, log_totals, delta, kv_list, heads, before, ties):
    own = before is not None
    rows = query.shape[0]
    width = query.shape[1] // heads
    slots = len(kv_list)
    scale = width**-0.5
    kernel = functools.partial(
        backward_kernel, own, slots, len(ties), rows // 2, math.log2(math.e) * scale, scale
    )
    head_spec = pl.BlockSpec((rows, width), lambda h, p: (0, h))
    line_spec = pl.BlockSpec((1, 1, rows), lambda h, p: (h, 0, 0))
    kv_spec = pl.BlockSpec((rows, 2 * width), lambda h, p: (0, 0))
    return pl.pallas_call(
        kernel,
        grid_spec=pltpu.PrefetchScalarGridSpec(
            num_scalar_prefetch=1,
            grid=(heads,),
            in_specs=[head_spec, head_spec, line_spec, line_spec]
            + [kv_spec] * slots
            + ([head_spec] if own else [])
            + [pl.BlockSpec(memory_space=pl.ANY)] * len(ties),
            out_specs=[head_spec] + [kv_spec] * slots,
            scratch_shapes=[
                pltpu.VMEM((rows, width), jnp.float32),
                pltpu.VMEM((slots, rows, 2 * width), jnp.float32),
            ],
        ),
        out_shape=[jax.ShapeDtypeStruct(query.shape, jnp.bfloat16 if own else jnp.float32)]
        + [jax.ShapeDtypeStruct((rows, 2 * width), jnp.bfloat16)] * slots,
        compiler_params=pltpu.CompilerParams(vmem_limit_bytes=48 * 2**20),
        cost_estimate=pl.CostEstimate(
            flops=20 * slots * heads * rows * rows * width,
            bytes_accessed=12 * rows * width * heads,
            transcendentals=slots * heads * rows * rows,
        ),
    )(place, query, grad_rows, log_totals, delta, *kv_list, *([before] if own else []), *ties)


def up_pairs(shift):
    return [(i, i + shift) for i in range(lax.axis_size("seq") - shift)]


def down_pairs(shift):
    return [(i + shift, i) for i in range(lax.axis_size("seq") - shift)]


def mm(left, right):
    return jnp.dot(left, right, preferred_element_type=jnp.float32)


def mm_nt(left, right):
    return f32_dot(left, right, 1, 1)


def mm_tn(left, right):
    return f32_dot(left, right, 0, 0)


def per_device(
    block_in,
    query_weight,
    key_weight,
    value_weight,
    output_weight,
    gate_weight,
    up_weight,
    down_weight,
    attention_norm,
    query_norm,
    key_norm,
    post_attention_norm,
    feedforward_norm,
    post_feedforward_norm,
    grad_out,
):
    parts = lax.axis_size("fsdp")
    gains = (
        attention_norm,
        query_norm,
        key_norm,
        post_attention_norm,
        feedforward_norm,
        post_feedforward_norm,
    )
    gain_sizes = [g.shape[0] for g in gains]
    gain_total = sum(gain_sizes)
    kv_rows, kv_width = key_weight.shape[0], 2 * key_weight.shape[1]
    kv_block = jnp.concatenate([key_weight, value_weight], 1)
    extra_rows = 16
    gain_block = jnp.concatenate(
        gains + (jnp.zeros((extra_rows * kv_width - gain_total,), jnp.bfloat16),)
    ).reshape(extra_rows, kv_width)
    kv_gathered = gather_rows(jnp.concatenate([kv_block, gain_block], 0), False)
    query_full = gather_rows(query_weight, True).reshape(-1, query_weight.shape[1])
    kv_full = kv_gathered[:, :kv_rows].reshape(-1, kv_width)
    gain_rows = kv_gathered[:, kv_rows:].reshape(parts, -1).astype(jnp.float32)
    split_gains = []
    offset = 0
    for size in gain_sizes:
        split_gains.append(gain_rows[:, offset : offset + size].reshape(-1))
        offset += size
    attention_gain, query_gain, key_gain, post_attention_gain, second_gain, post_second_gain = (
        split_gains
    )
    late = lax.optimization_barrier(
        (output_weight, gate_weight, up_weight, down_weight, kv_gathered)
    )[:4]
    directions = (True, True, False, False)
    late = [gather_steps(gather_start(w), d, 0, -1) for w, d in zip(late, directions)]

    token_count = block_in.shape[0]
    head_size = query_gain.shape[0]
    head_count = query_full.shape[1] // head_size
    slots = lax.axis_size("seq")
    seq_place = lax.axis_index("seq")
    place = seq_place.astype(jnp.int32).reshape(1)
    input_f = block_in.astype(jnp.float32)
    normed, pull_normed = jax.vjp(rms_scale, input_f, attention_gain)
    normed_low = normed.astype(jnp.bfloat16)
    kv_lin = mm(normed_low, kv_full)
    key_lin = kv_lin[:, :head_size]
    value_low = kv_lin[:, head_size:].astype(jnp.bfloat16)
    positions = (seq_place * token_count + jnp.arange(token_count, dtype=jnp.int32)).astype(
        jnp.float32
    )
    cosine_table, sine_table = angles_for(positions, head_size)

    def query_piece(values, gain_row):
        return rotate(rms_scale(values, gain_row), cosine_table[:, None, :], sine_table[:, None, :])

    def key_piece(values, gain_row):
        return rotate(rms_scale(values, gain_row), cosine_table, sine_table)

    key_rows, pull_keys = jax.vjp(key_piece, key_lin, key_gain)
    kv_own = jnp.concatenate([key_rows.astype(jnp.bfloat16), value_low], 1)
    kv_list = [kv_own] + [lax.ppermute(kv_own, "seq", up_pairs(s)) for s in range(1, slots)]
    query_lin = mm(normed_low, query_full).reshape(token_count, head_count, head_size)
    queries, pull_queries = jax.vjp(query_piece, query_lin, query_gain)
    queries_low = queries.astype(jnp.bfloat16).reshape(token_count, head_count * head_size)
    before = attend_forward(place, queries_low, kv_list[:1], head_count, None, [])
    mixed, totals = attend_forward(
        place, queries_low, kv_list[1:], head_count, before, late
    )
    order_length = len(gather_order("fsdp", True))
    output_full, gate_full, up_full, down_full = (
        gather_steps(w, d, order_length - 1, None).reshape(-1, w.shape[-1])
        for w, d in zip(late, directions)
    )
    attended = mm(mixed, output_full)
    post_branch, pull_post = jax.vjp(rms_scale, attended, post_attention_gain)
    residual = input_f + post_branch
    normed_second, pull_second = jax.vjp(rms_scale, residual, second_gain)
    second_low = normed_second.astype(jnp.bfloat16)
    gate_lin = mm(second_low, gate_full)
    up_lin = mm(second_low, up_full)
    activated, pull_activated = jax.vjp(gelu_product, gate_lin, up_lin)
    activated_low = activated.astype(jnp.bfloat16)
    down_lin = mm(activated_low, down_full)
    tail_branch, pull_tail = jax.vjp(rms_scale, down_lin, post_second_gain)
    block_out = (residual + tail_branch).astype(jnp.bfloat16)
    grad_f = grad_out.astype(jnp.float32)
    grad_down, grad_post_second = pull_tail(grad_f)
    grad_down_low = grad_down.astype(jnp.bfloat16)

    def product(left, right):
        return mm_tn(left, right).astype(jnp.bfloat16).reshape(parts, -1, right.shape[1])

    sum_down = scatter_steps(
        scatter_start(product(activated_low, grad_down_low)), False, 0, -1
    )
    grad_activated = mm_nt(grad_down_low, down_full)
    grad_gate, grad_up = pull_activated(grad_activated)
    gate_low = grad_gate.astype(jnp.bfloat16)
    up_low = grad_up.astype(jnp.bfloat16)
    pair_product = jnp.concatenate(
        [product(second_low, gate_low), product(second_low, up_low)], 2
    )
    sum_pair = scatter_steps(scatter_start(pair_product), True, 0, 1)
    grad_second = mm_nt(gate_low, gate_full) + mm_nt(up_low, up_full)
    grad_resid_part, grad_second_gain = pull_second(grad_second)
    grad_residual = grad_f + grad_resid_part
    grad_attended, grad_post_attention = pull_post(grad_residual)
    attended_low = grad_attended.astype(jnp.bfloat16)
    sum_output = scatter_start(product(mixed, attended_low))
    grad_mixed = mm_nt(attended_low, output_full).astype(jnp.bfloat16)
    delta = jnp.sum(
        (grad_mixed.astype(jnp.float32) * mixed.astype(jnp.float32)).reshape(
            token_count, head_count, head_size
        ),
        -1,
    ).T.reshape(head_count, 1, token_count)
    outs = attend_backward(
        place,
        queries_low,
        grad_mixed,
        jnp.log2(totals),
        delta,
        kv_list[1:],
        head_count,
        None,
        [sum_down, sum_pair],
    )
    sum_down = scatter_end(scatter_steps(sum_down, False, -1 % order_length, None))
    sum_pair = scatter_steps(sum_pair, True, 1, -1)
    sum_output = scatter_steps(sum_output, False, 0, -1)
    own_outs = attend_backward(
        place,
        queries_low,
        grad_mixed,
        jnp.log2(totals),
        delta,
        kv_list[:1],
        head_count,
        outs[0],
        [sum_down, sum_pair, sum_output],
    )
    sum_pair = scatter_end(scatter_steps(sum_pair, True, -1 % order_length, None))
    sum_output = scatter_end(scatter_steps(sum_output, False, -1 % order_length, None))
    grad_queries, kv_grads = own_outs[0], list(own_outs[1:]) + list(outs[1:])
    kv_grad = kv_grads[0].astype(jnp.float32)
    for shift in range(1, slots):
        arrived = lax.ppermute(kv_grads[shift], "seq", down_pairs(shift))
        kv_grad = kv_grad + arrived.astype(jnp.float32)
    kv_grad = kv_grad.astype(jnp.bfloat16)
    grad_query_lin, grad_query_gain = pull_queries(
        grad_queries.astype(jnp.float32).reshape(query_lin.shape)
    )
    query_lin_low = grad_query_lin.reshape(token_count, head_count * head_size).astype(jnp.bfloat16)
    sum_query = scatter_end(
        scatter_steps(scatter_start(product(normed_low, query_lin_low)), True, 0, None)
    )
    grad_normed = mm_nt(query_lin_low, query_full)
    grad_key_lin, grad_key_gain = pull_keys(kv_grad[:, :head_size].astype(jnp.float32))
    kv_lin_low = jnp.concatenate(
        [grad_key_lin.astype(jnp.bfloat16), kv_grad[:, head_size:]], 1
    )
    grad_normed = grad_normed + mm_nt(kv_lin_low, kv_full)
    grad_input_part, grad_attention_gain = pull_normed(grad_normed)
    grad_in = (grad_residual + grad_input_part).astype(jnp.bfloat16)
    gain_grads = (
        grad_attention_gain,
        grad_query_gain,
        grad_key_gain,
        grad_post_attention,
        grad_second_gain,
        grad_post_second,
    )
    gain_grad_rows = jnp.concatenate(
        [g.astype(jnp.bfloat16).reshape(parts, -1) for g in gain_grads]
        + [jnp.zeros((parts, extra_rows * kv_width - gain_total), jnp.bfloat16)],
        1,
    ).reshape(parts, extra_rows, kv_width)
    kv_product = mm_tn(normed_low, kv_lin_low).astype(jnp.bfloat16).reshape(
        parts, kv_rows, kv_width
    )
    sum_kv = scatter_end(
        scatter_steps(
            scatter_start(jnp.concatenate([kv_product, gain_grad_rows], 1)), False, 0, None
        )
    )

    down_sum = seq_sum(sum_down).astype(jnp.float32)
    pair_sum = seq_sum(sum_pair).astype(jnp.float32)
    half = pair_sum.shape[1] // 2
    gate_sum, up_sum = pair_sum[:, :half], pair_sum[:, half:]
    output_sum = seq_sum(sum_output).astype(jnp.float32)
    query_sum = seq_sum(sum_query).astype(jnp.float32)
    kv_sum = seq_sum(sum_kv).astype(jnp.float32)
    gain_sum = kv_sum[kv_rows:].reshape(-1)
    gain_outs = []
    offset = 0
    for size in gain_sizes:
        gain_outs.append(gain_sum[offset : offset + size])
        offset += size
    return (
        block_out,
        grad_in,
        query_sum,
        kv_sum[:kv_rows, :head_size],
        kv_sum[:kv_rows, head_size:],
        output_sum,
        gate_sum,
        up_sum,
        down_sum,
        *gain_outs,
    )


def solution(mesh):
    in_specs = (
        P(("fsdp", "seq"), None),
        P("fsdp", None),
        P("fsdp", None),
        P("fsdp", None),
        P("fsdp", None),
        P("fsdp", None),
        P("fsdp", None),
        P("fsdp", None),
        P("fsdp"),
        P("fsdp"),
        P("fsdp"),
        P("fsdp"),
        P("fsdp"),
        P("fsdp"),
        P(("fsdp", "seq"), None),
    )
    out_specs = (
        P(("fsdp", "seq"), None),
        P(("fsdp", "seq"), None),
        P("fsdp", None),
        P("fsdp", None),
        P("fsdp", None),
        P("fsdp", None),
        P("fsdp", None),
        P("fsdp", None),
        P("fsdp", None),
        P("fsdp"),
        P("fsdp"),
        P("fsdp"),
        P("fsdp"),
        P("fsdp"),
        P("fsdp"),
    )
    return jax.shard_map(
        per_device, mesh=mesh, in_specs=in_specs, out_specs=out_specs, check_vma=False
    )
```
